32 devices in a mesh: groups: 2 (over y), dp: 4 (over z), tensor: 4 (over x, core).
Axes of the slice: x: 2, y: 2, z: 4, core: 2. Of those that a mesh axis runs over, the one named last changes fastest.
Arguments:
- entered_tokens: bfloat16 [1024, 8192], P(('groups', 'dp'), 'tensor'), parts along dimension 0, may hold values from -6 to 6
- output_grad: bfloat16 [1024, 1024], P(('groups', 'dp'), 'tensor'), parts along dimension 0, may hold values from -6 to 6
- value_matrix: bfloat16 [8192, 1024], P(None, 'tensor'), may hold values from -0.0625 to 0.0625
- adapter_down: bfloat16 [16, 16, 8192], P(('groups', 'dp'), None, 'tensor'), parts along dimension 0, may hold values from -0.0625 to 0.0625
- adapter_up: bfloat16 [16, 16, 1024], P(('groups', 'dp'), None, 'tensor'), parts along dimension 0, may hold values from -1.5 to 1.5
- segment_owner_adapter: int32 [8], P('groups'), parts along dimension 0, may hold values from 0 to 7, as said below
- adapter_storage: int32 [16], P('groups'), parts along dimension 0, may hold values from 0 to 7, as said below
Outputs:
- layer_input_grad: bfloat16 [1024, 8192], P(('groups', 'dp'), 'tensor'), parts along dimension 0
- grad_down: float32 [16, 16, 8192], P(('groups', 'dp'), None, 'tensor'), parts along dimension 0
- grad_up: float32 [16, 16, 1024], P(('groups', 'dp'), None, 'tensor'), parts along dimension 0
The draws below stay inside these ranges and needn't reach their ends.
There are 2 independent parts, one for each index of `groups`. The reference program is written for one: setup_inputs(seed, part) draws one part's arguments, and reference() takes and returns one part's arrays. A program takes and returns all parts, laid end to end along the dimension named above; an argument that names none is the same for every part. Nothing has to cross between parts.
Inputs may be any that keep to these rules, and one draw needn't show every extreme that they name: `segment_owner_adapter`: adapter ids of segments; every index of dp stores the adapter of at least one segment. `adapter_storage`: A permutation: each slot holds exactly one adapter.
All inputs are finite; a program needn't handle non-finite values.
Results may differ from the reference program's by a relative error of at most 0.001.
Values may be sent and summed in bfloat16 or wider, within the bound.
A program may use at most 64 MiB of HBM per device.

```python
import jax
import jax.numpy as jnp
from jax import lax

MODEL_WIDTH = 8192
VALUE_OUT_WIDTH = 1024
ADAPTER_RANK = 16
SEGMENT_TOKENS = 128
TOK_DEV = 128
TOKENS = 512
SEGMENTS = 4
ADAPTER_TOTAL = 8


def place_value(order_map, position, wanted):
    holder = jnp.argmax(order_map == wanted)
    old_value = order_map[position]
    return order_map.at[holder].set(old_value).at[position].set(wanted)


def shared_tables(key):
    seg_dev = TOK_DEV // SEGMENT_TOKENS
    owners = SEGMENTS // seg_dev
    per_holder = ADAPTER_TOTAL // owners
    half_way = owners // 2
    slot_of = jax.random.permutation(jax.random.fold_in(key, 11), ADAPTER_TOTAL).astype(jnp.int32)
    adapter_at = jnp.argsort(slot_of, stable=True).astype(jnp.int32)
    order_map = jax.random.permutation(jax.random.fold_in(key, 12), owners).astype(jnp.int32)
    centre = jax.random.randint(jax.random.fold_in(key, 13), (), 0, owners, dtype=jnp.int32)
    order_map = place_value(order_map, centre, (centre + half_way) % owners)
    order_map = place_value(order_map, (centre + 1) % owners, centre)
    order_map = place_value(order_map, (centre + 2) % owners, (centre + 3) % owners)
    choose_one = jax.random.randint(jax.random.fold_in(key, 14), (owners,), 0, per_holder, dtype=jnp.int32)
    first_seg = jnp.take(adapter_at, order_map * per_holder + choose_one)
    draw_one = jax.random.randint(jax.random.fold_in(key, 15), (owners, seg_dev - 1), 0, ADAPTER_TOTAL, dtype=jnp.int32)
    draw_two = jax.random.randint(jax.random.fold_in(key, 16), (owners, seg_dev - 1), 0, ADAPTER_TOTAL, dtype=jnp.int32)
    more_segs = jnp.minimum(draw_one, draw_two)
    segments = jnp.concatenate([first_seg[:, None], more_segs], axis=1).reshape(-1)
    return (slot_of, segments.astype(jnp.int32))


def draw_segment_owner_adapter(key, part):
    slot_of, segments = shared_tables(key)
    return segments


def draw_adapter_storage(key, part):
    slot_of, segments = shared_tables(key)
    return slot_of


def level_of(rng, dims, cuts, smallest, top_value):
    loudness = 1.0
    for dim, blocks in cuts:
        heights = jax.random.uniform(jax.random.fold_in(jax.random.fold_in(rng, 6), dim), (blocks,), jnp.float32, smallest / len(cuts), top_value / len(cuts))
        loudness = loudness * jnp.repeat(jnp.exp(heights), dims[dim] // blocks).reshape((-1,) + (1,) * (len(dims) - 1 - dim))
    return loudness


def gaussian(key, extent, deviation, most, cuts=(), held_as=jnp.bfloat16):
    result = deviation * jax.random.normal(key, extent, jnp.float32)
    if cuts:
        result = result * level_of(key, extent, cuts, -0.22, 0.18)
    return jnp.clip(result, -most, most).astype(held_as)


def setup_inputs(seed: int = 0, part: int = 0) -> dict:
    key_list = jax.random.split(jax.random.key(seed), 8)
    own_keys = jax.random.split(jax.random.fold_in(key_list[7], part), 8)
    return {
        "entered_tokens": gaussian(own_keys[0], (TOKENS, MODEL_WIDTH), 1.0, 6.0, ((0, 4), (1, 4))),
        "output_grad": gaussian(own_keys[1], (TOKENS, VALUE_OUT_WIDTH), 1.0, 6.0, ((0, 4), (1, 4))),
        "value_matrix": gaussian(key_list[2], (MODEL_WIDTH, VALUE_OUT_WIDTH), MODEL_WIDTH ** -0.5, 0.0625, ((1, 4),)),
        "adapter_down": gaussian(own_keys[3], (ADAPTER_TOTAL, ADAPTER_RANK, MODEL_WIDTH), MODEL_WIDTH ** -0.5, 0.0625, ((0, 4), (2, 4))),
        "adapter_up": gaussian(own_keys[4], (ADAPTER_TOTAL, ADAPTER_RANK, VALUE_OUT_WIDTH), ADAPTER_RANK ** -0.5, 1.5, ((0, 4), (2, 4))),
        "segment_owner_adapter": draw_segment_owner_adapter(jax.random.fold_in(jax.random.fold_in(key_list[7], part), 71), part),
        "adapter_storage": draw_adapter_storage(jax.random.fold_in(jax.random.fold_in(key_list[7], part), 71), part),
    }


adapter_scale = 2.0
exact_check = lax.Precision.HIGHEST


def reference(entered_tokens, output_grad, value_matrix, adapter_down, adapter_up, segment_owner_adapter, adapter_storage):
    segment_count = segment_owner_adapter.shape[0]
    segment_slots = jnp.take(adapter_storage, segment_owner_adapter)
    picked_down = jnp.take(adapter_down, segment_slots, axis=0).astype(jnp.float32)
    picked_up = jnp.take(adapter_up, segment_slots, axis=0).astype(jnp.float32)
    seg_input = entered_tokens.reshape(segment_count, SEGMENT_TOKENS, MODEL_WIDTH).astype(jnp.float32)
    seg_grad = output_grad.reshape(segment_count, SEGMENT_TOKENS, VALUE_OUT_WIDTH).astype(jnp.float32)
    low_in = jnp.einsum("std,srd->str", seg_input, picked_down, precision=exact_check)
    rank_space_grad = jnp.einsum("stk,srk->str", seg_grad, picked_up, precision=exact_check)
    frozen_grad = jnp.dot(output_grad, value_matrix.T, preferred_element_type=jnp.float32)
    adapter_term = adapter_scale * jnp.einsum("mgu,mue->mge", rank_space_grad, picked_down, precision=exact_check)
    layer_input_grad = (frozen_grad + adapter_term.reshape(segment_count * SEGMENT_TOKENS, MODEL_WIDTH)).astype(jnp.bfloat16)
    adapter_hits = segment_owner_adapter[:, None] == jnp.arange(ADAPTER_TOTAL, dtype=jnp.int32)[None, :]
    segment_counts = SEGMENT_TOKENS * jnp.sum(adapter_hits.astype(jnp.int32), axis=0)
    scale_factor = adapter_scale / jnp.maximum(segment_counts, SEGMENT_TOKENS).astype(jnp.float32)
    hit_weight = adapter_hits.astype(jnp.float32)
    down_terms = jnp.einsum("str,std->srd", rank_space_grad, seg_input, precision=exact_check)
    up_terms = jnp.einsum("str,stk->srk", low_in, seg_grad, precision=exact_check)
    down_sums = jnp.einsum("sa,srd->ard", hit_weight, down_terms, precision=exact_check) * scale_factor[:, None, None]
    up_sums = jnp.einsum("sa,srk->ark", hit_weight, up_terms, precision=exact_check) * scale_factor[:, None, None]
    grad_down = jnp.zeros((ADAPTER_TOTAL, ADAPTER_RANK, MODEL_WIDTH), jnp.float32).at[adapter_storage].set(down_sums)
    grad_up = jnp.zeros((ADAPTER_TOTAL, ADAPTER_RANK, VALUE_OUT_WIDTH), jnp.float32).at[adapter_storage].set(up_sums)
    return layer_input_grad, grad_down, grad_up
```

```python
import functools

import jax
import jax.numpy as jnp
from jax import lax
from jax.experimental import pallas as pl
from jax.experimental.pallas import tpu as pltpu
from jax.sharding import PartitionSpec as P

SEGMENT_TOKENS = 128
CORES = 2
adapter_scale = 2.0
EARLY = 2
MESH = pl.DeviceIdType.MESH
F32 = jnp.float32
BF16 = jnp.bfloat16


def dot_last(a, b):
    return lax.dot_general(a, b, (((1,), (1,)), ((), ())), preferred_element_type=F32)


def three_parts(x, axis):
    high = x.astype(BF16)
    rest = x - high.astype(F32)
    mid = rest.astype(BF16)
    low = (rest - mid.astype(F32)).astype(BF16)
    return jnp.concatenate([high, mid, low], axis=axis)


def add_parts(x, rows):
    return x[:rows] + x[rows : 2 * rows] + x[2 * rows :]


def kernel(
    n,
    tn,
    chunk,
    seg_ref,
    store_ref,
    tok_ref,
    grad_ref,
    w_ref,
    down_ref,
    up_ref,
    out_ref,
    gdown_ref,
    gup_ref,
    w_mine,
    w_sib,
    g_sib,
    abuf,
    lbuf,
    tbuf,
    psend,
    prec,
    acc,
    w_sem,
    ws_send,
    ws_recv,
    g_sem,
    a_send,
    a_recv,
    l_send,
    l_recv,
    t_send,
    t_recv,
    p_send,
    p_recv,
):
    per, rank, feat = down_ref.shape
    cols = up_ref.shape[2]
    chips = tn // CORES
    chunks = feat // chunk
    z = lax.axis_index("dp")
    j = lax.axis_index("tensor")
    x = j // CORES
    c = lax.rem(j, CORES)
    sib = x * CORES + (1 - c)

    def w_rows(chip, core, i):
        start = (chip * CORES + core) * feat + i * chunk
        return w_ref.at[pl.ds(pl.multiple_of(start, chunk), chunk)]

    steps = [(s, i) for s in list(range(1, chips)) + [0] for i in range(chunks)]

    w_local = {}
    for s, i in steps:
        chip = lax.rem(x + s, chips)
        w_local[s, i] = pltpu.make_async_copy(
            w_rows(chip, c, i), w_mine.at[s, pl.ds(i * chunk, chunk)], w_sem.at[s, i]
        )
        w_local[s, i].start()

    barrier = pltpu.get_barrier_semaphore()
    for s in range(1, tn):
        pl.semaphore_signal(
            barrier, inc=1, device_id={"tensor": lax.rem(j + s, tn)}, device_id_type=MESH
        )
    for s in range(1, n):
        pl.semaphore_signal(
            barrier, inc=1, device_id={"dp": lax.rem(z + s, n)}, device_id_type=MESH
        )

    my_slot = store_ref[seg_ref[z]]
    my_owner = my_slot // per
    kept = jnp.int32(0)
    user = jnp.int32(0)
    hits = jnp.int32(0)
    for s in range(n):
        slot = store_ref[seg_ref[s]]
        here = slot // per == z
        kept = jnp.where(here, lax.rem(slot, per), kept)
        user = jnp.where(here, s, user)
        hits = hits + jnp.where(seg_ref[s] == seg_ref[z], SEGMENT_TOKENS, 0)
    from_owner = lax.rem(z - my_owner + n, n)
    from_user = lax.rem(z - user + n, n)

    abuf[0, :, :feat] = down_ref[kept]
    abuf[0, :, feat:] = up_ref[kept]

    pl.semaphore_wait(barrier, (tn - 1) + (n - 1))

    a_copies = []
    for s in range(1, n):
        cp = pltpu.make_async_remote_copy(
            src_ref=abuf.at[0],
            dst_ref=abuf.at[s],
            send_sem=a_send.at[s - 1],
            recv_sem=a_recv.at[s - 1],
            device_id={"dp": lax.rem(z + s, n)},
            device_id_type=MESH,
        )
        cp.start()
        a_copies.append(cp)
    g_copy = pltpu.make_async_remote_copy(
        src_ref=grad_ref,
        dst_ref=g_sib,
        send_sem=g_sem.at[0],
        recv_sem=g_sem.at[1],
        device_id={"tensor": sib},
        device_id_type=MESH,
    )
    g_copy.start()
    w_copies = {}
    for s, i in steps:
        chip = lax.rem(x + s, chips)
        cp = pltpu.make_async_remote_copy(
            src_ref=w_rows(chip, 1 - c, i),
            dst_ref=w_sib.at[s, pl.ds(i * chunk, chunk)],
            send_sem=ws_send.at[s, i],
            recv_sem=ws_recv.at[s, i],
            device_id={"tensor": sib},
            device_id_type=MESH,
        )
        cp.start()
        w_copies[s, i] = cp

    def product(s, i):
        w_local[s, i].wait()
        w_copies[s, i].wait_recv()
        rows = pl.ds(i * chunk, chunk)
        return dot_last(grad_ref[...], w_mine[s, rows]) + dot_last(g_sib[...], w_sib[s, rows])

    p_copies = {}

    def send_partial(s, i):
        psend[s - 1, i] = product(s, i)
        cp = pltpu.make_async_remote_copy(
            src_ref=psend.at[s - 1, i],
            dst_ref=prec.at[s - 1, i],
            send_sem=p_send.at[s - 1, i],
            recv_sem=p_recv.at[s - 1, i],
            device_id={"tensor": lax.rem(x + s, chips) * CORES + c},
            device_id_type=MESH,
        )
        cp.start()
        p_copies[s, i] = cp

    partials = [(s, i) for s, i in steps if s > 0]
    g_copy.wait_recv()
    for s, i in partials[:EARLY]:
        send_partial(s, i)

    for cp in a_copies:
        cp.wait_recv()
    lbuf[0, :rank] = dot_last(abuf[from_owner, :, :feat], tok_ref[...])
    lbuf[0, rank:] = dot_last(abuf[from_owner, :, feat:], grad_ref[...])
    l_copies = []
    for s in range(1, tn):
        cp = pltpu.make_async_remote_copy(
            src_ref=lbuf.at[0],
            dst_ref=lbuf.at[s],
            send_sem=l_send.at[s - 1],
            recv_sem=l_recv.at[s - 1],
            device_id={"tensor": lax.rem(j + s, tn)},
            device_id_type=MESH,
        )
        cp.start()
        l_copies.append(cp)
    for s, i in partials[EARLY:]:
        send_partial(s, i)
    for cp in l_copies:
        cp.wait_recv()
    low = lbuf[0]
    for s in range(1, tn):
        low = low + lbuf[s]
    low_in = low[:rank]
    low_grad = low[rank:]

    limit = jnp.maximum(hits, SEGMENT_TOKENS).astype(F32)
    factor = adapter_scale / jnp.full((rank, SEGMENT_TOKENS), limit, F32)
    grad_parts = three_parts(low_grad * factor, 0)
    in_parts = three_parts(low_in * factor, 0)
    tbuf[0, :, :feat] = add_parts(
        jnp.dot(grad_parts, tok_ref[...], preferred_element_type=F32), rank
    )
    tbuf[0, :, feat:] = add_parts(
        jnp.dot(in_parts, grad_ref[...], preferred_element_type=F32), rank
    )
    t_copies = []
    for s in range(1, n):
        cp = pltpu.make_async_remote_copy(
            src_ref=tbuf.at[0],
            dst_ref=tbuf.at[s],
            send_sem=t_send.at[s - 1],
            recv_sem=t_recv.at[s - 1],
            device_id={"dp": lax.rem(z + s, n)},
            device_id_type=MESH,
        )
        cp.start()
        t_copies.append(cp)

    left = three_parts(jnp.transpose(adapter_scale * low_grad), 1)
    for i in range(chunks):
        span = pl.ds(i * chunk, chunk)
        down = abuf[from_owner, :, span]
        acc[i] = product(0, i) + jnp.dot(
            left, jnp.concatenate([down, down, down], axis=0), preferred_element_type=F32
        )
    for i in range(chunks):
        total = acc[i]
        for s in range(1, chips):
            p_copies[s, i].wait_recv()
            total = total + prec[s - 1, i]
        out_ref[:, pl.ds(i * chunk, chunk)] = total.astype(BF16)

    for cp in t_copies:
        cp.wait_recv()
    for k in range(per):
        mine = jnp.where(kept == k, 1.0, 0.0).astype(F32)
        gdown_ref[k] = tbuf[from_user, :, :feat] * mine
        gup_ref[k] = tbuf[from_user, :, feat:] * mine

    g_copy.wait_send()
    for group in (a_copies, l_copies, t_copies, w_copies.values(), p_copies.values()):
        for cp in group:
            cp.wait_send()


def on_device(
    n,
    tn,
    entered_tokens,
    output_grad,
    value_matrix,
    adapter_down,
    adapter_up,
    segment_owner_adapter,
    adapter_storage,
):
    tokens, feat = entered_tokens.shape
    cols = output_grad.shape[1]
    per, rank, _ = adapter_down.shape
    assert tokens == SEGMENT_TOKENS and segment_owner_adapter.shape[0] == n
    chips = tn // CORES
    chunk = min(512, feat)
    chunks = feat // chunk
    vmem = pl.BlockSpec(memory_space=pltpu.VMEM)
    smem = pl.BlockSpec(memory_space=pltpu.SMEM)
    dma = pltpu.SemaphoreType.DMA
    return pl.pallas_call(
        functools.partial(kernel, n, tn, chunk),
        out_shape=(
            jax.ShapeDtypeStruct((tokens, feat), BF16),
            jax.ShapeDtypeStruct((per, rank, feat), F32),
            jax.ShapeDtypeStruct((per, rank, cols), F32),
        ),
        in_specs=[smem, smem, vmem, vmem, pl.BlockSpec(memory_space=pl.ANY), vmem, vmem],
        out_specs=(vmem, vmem, vmem),
        scratch_shapes=[
            pltpu.VMEM((chips, feat, cols), BF16),
            pltpu.VMEM((chips, feat, cols), BF16),
            pltpu.VMEM((tokens, cols), BF16),
            pltpu.VMEM((n, rank, feat + cols), BF16),
            pltpu.VMEM((tn, 2 * rank, tokens), F32),
            pltpu.VMEM((n, rank, feat + cols), F32),
            pltpu.VMEM((chips - 1, chunks, tokens, chunk), F32),
            pltpu.VMEM((chips - 1, chunks, tokens, chunk), F32),
            pltpu.VMEM((chunks, tokens, chunk), F32),
            dma((chips, chunks)),
            dma((chips, chunks)),
            dma((chips, chunks)),
            dma((2,)),
            dma((n - 1,)),
            dma((n - 1,)),
            dma((tn - 1,)),
            dma((tn - 1,)),
            dma((n - 1,)),
            dma((n - 1,)),
            dma((chips - 1, chunks)),
            dma((chips - 1, chunks)),
        ],
        compiler_params=pltpu.CompilerParams(
            collective_id=0, has_side_effects=True, vmem_limit_bytes=40 * 1024 * 1024
        ),
        cost_estimate=pl.CostEstimate(
            flops=2 * tokens * feat * cols * tn, bytes_accessed=2 * value_matrix.size, transcendentals=0
        ),
    )(
        segment_owner_adapter,
        adapter_storage,
        entered_tokens,
        output_grad,
        value_matrix,
        adapter_down,
        adapter_up,
    )


def solution(mesh):
    in_specs = (
        P(("groups", "dp"), "tensor"),
        P(("groups", "dp"), "tensor"),
        P(None, "tensor"),
        P(("groups", "dp"), None, "tensor"),
        P(("groups", "dp"), None, "tensor"),
        P("groups"),
        P("groups"),
    )
    out_specs = (
        P(("groups", "dp"), "tensor"),
        P(("groups", "dp"), None, "tensor"),
        P(("groups", "dp"), None, "tensor"),
    )
    body = functools.partial(on_device, mesh.shape["dp"], mesh.shape["tensor"])
    return jax.shard_map(
        body, mesh=mesh, in_specs=in_specs, out_specs=out_specs, check_vma=False
    )
```

```python
import functools

import jax
import jax.numpy as jnp
from jax import lax
from jax.experimental import pallas as pl
from jax.experimental.pallas import tpu as pltpu
from jax.sharding import PartitionSpec as P

SEGMENT_TOKENS = 128
CORES = 2
adapter_scale = 2.0
VMEM_LIMIT = 60 * 1024 * 1024
EARLY = 2
MESH = pl.DeviceIdType.MESH
F32 = jnp.float32
BF16 = jnp.bfloat16


def dot_last(a, b):
    return lax.dot_general(a, b, (((1,), (1,)), ((), ())), preferred_element_type=F32)


def three_parts(x, axis):
    high = x.astype(BF16)
    rest = x - high.astype(F32)
    mid = rest.astype(BF16)
    low = (rest - mid.astype(F32)).astype(BF16)
    return jnp.concatenate([high, mid, low], axis=axis)


def add_parts(x, rows):
    return x[:rows] + x[rows : 2 * rows] + x[2 * rows :]


def kernel(
    n,
    tn,
    chunk,
    seg_hbm,
    store_hbm,
    tok_hbm,
    grad_hbm,
    w_ref,
    down_hbm,
    up_hbm,
    out_ref,
    gdown_ref,
    gup_ref,
    seg_ref,
    store_ref,
    tok_ref,
    grad_ref,
    down_ref,
    up_ref,
    in_sem,
    w_mine,
    w_sib,
    g_sib,
    abuf,
    lbuf,
    tbuf,
    psend,
    prec,
    acc,
    w_sem,
    ws_send,
    ws_recv,
    g_sem,
    a_send,
    a_recv,
    l_send,
    l_recv,
    t_send,
    t_recv,
    p_send,
    p_recv,
):
    per, rank, feat = down_ref.shape
    cols = up_ref.shape[2]
    chips = tn // CORES
    chunks = feat // chunk
    z = lax.axis_index("dp")
    j = lax.axis_index("tensor")
    x = j // CORES
    c = lax.rem(j, CORES)
    sib = x * CORES + (1 - c)

    def w_rows(chip, core, i):
        start = (chip * CORES + core) * feat + i * chunk
        return w_ref.at[pl.ds(pl.multiple_of(start, chunk), chunk)]

    loads = [
        pltpu.make_async_copy(src, dst, in_sem.at[k])
        for k, (src, dst) in enumerate(
            (
                (seg_hbm, seg_ref),
                (store_hbm, store_ref),
                (down_hbm, down_ref),
                (up_hbm, up_ref),
                (grad_hbm, grad_ref),
                (tok_hbm, tok_ref),
            )
        )
    ]
    for cp in loads:
        cp.start()

    steps = [(s, i) for s in list(range(1, chips)) + [0] for i in range(chunks)]

    w_local = {}
    for s, i in steps:
        chip = lax.rem(x + s, chips)
        w_local[s, i] = pltpu.make_async_copy(
            w_rows(chip, c, i), w_mine.at[s, pl.ds(i * chunk, chunk)], w_sem.at[s, i]
        )
        w_local[s, i].start()

    barrier = pltpu.get_barrier_semaphore()
    for s in range(1, tn):
        pl.semaphore_signal(
            barrier, inc=1, device_id={"tensor": lax.rem(j + s, tn)}, device_id_type=MESH
        )
    for s in range(1, n):
        pl.semaphore_signal(
            barrier, inc=1, device_id={"dp": lax.rem(z + s, n)}, device_id_type=MESH
        )

    for cp in loads[:4]:
        cp.wait()
    my_slot = store_ref[seg_ref[z]]
    my_owner = my_slot // per
    kept = jnp.int32(0)
    user = jnp.int32(0)
    hits = jnp.int32(0)
    for s in range(n):
        slot = store_ref[seg_ref[s]]
        here = slot // per == z
        kept = jnp.where(here, lax.rem(slot, per), kept)
        user = jnp.where(here, s, user)
        hits = hits + jnp.where(seg_ref[s] == seg_ref[z], SEGMENT_TOKENS, 0)
    from_owner = lax.rem(z - my_owner + n, n)
    from_user = lax.rem(z - user + n, n)

    abuf[0, :, :feat] = down_ref[kept]
    abuf[0, :, feat:] = up_ref[kept]

    pl.semaphore_wait(barrier, (tn - 1) + (n - 1))

    a_copies = []
    for s in range(1, n):
        cp = pltpu.make_async_remote_copy(
            src_ref=abuf.at[0],
            dst_ref=abuf.at[s],
            send_sem=a_send.at[s - 1],
            recv_sem=a_recv.at[s - 1],
            device_id={"dp": lax.rem(z + s, n)},
            device_id_type=MESH,
        )
        cp.start()
        a_copies.append(cp)
    loads[4].wait()
    g_copy = pltpu.make_async_remote_copy(
        src_ref=grad_ref,
        dst_ref=g_sib,
        send_sem=g_sem.at[0],
        recv_sem=g_sem.at[1],
        device_id={"tensor": sib},
        device_id_type=MESH,
    )
    g_copy.start()
    w_copies = {}
    for s, i in steps:
        chip = lax.rem(x + s, chips)
        cp = pltpu.make_async_remote_copy(
            src_ref=w_rows(chip, 1 - c, i),
            dst_ref=w_sib.at[s, pl.ds(i * chunk, chunk)],
            send_sem=ws_send.at[s, i],
            recv_sem=ws_recv.at[s, i],
            device_id={"tensor": sib},
            device_id_type=MESH,
        )
        cp.start()
        w_copies[s, i] = cp

    def product(s, i):
        w_local[s, i].wait()
        w_copies[s, i].wait_recv()
        rows = pl.ds(i * chunk, chunk)
        return dot_last(grad_ref[...], w_mine[s, rows]) + dot_last(g_sib[...], w_sib[s, rows])

    p_copies = {}

    def send_partial(s, i):
        psend[s - 1, i] = product(s, i)
        cp = pltpu.make_async_remote_copy(
            src_ref=psend.at[s - 1, i],
            dst_ref=prec.at[s - 1, i],
            send_sem=p_send.at[s - 1, i],
            recv_sem=p_recv.at[s - 1, i],
            device_id={"tensor": lax.rem(x + s, chips) * CORES + c},
            device_id_type=MESH,
        )
        cp.start()
        p_copies[s, i] = cp

    partials = [(s, i) for s, i in steps if s > 0]
    g_copy.wait_recv()
    for s, i in partials[:EARLY]:
        send_partial(s, i)

    loads[5].wait()
    for cp in a_copies:
        cp.wait_recv()
    lbuf[0, :rank] = dot_last(abuf[from_owner, :, :feat], tok_ref[...])
    lbuf[0, rank:] = dot_last(abuf[from_owner, :, feat:], grad_ref[...])
    l_copies = []
    for s in range(1, tn):
        cp = pltpu.make_async_remote_copy(
            src_ref=lbuf.at[0],
            dst_ref=lbuf.at[s],
            send_sem=l_send.at[s - 1],
            recv_sem=l_recv.at[s - 1],
            device_id={"tensor": lax.rem(j + s, tn)},
            device_id_type=MESH,
        )
        cp.start()
        l_copies.append(cp)
    for s, i in partials[EARLY:]:
        send_partial(s, i)
    for cp in l_copies:
        cp.wait_recv()
    low = lbuf[0]
    for s in range(1, tn):
        low = low + lbuf[s]
    low_in = low[:rank]
    low_grad = low[rank:]

    limit = jnp.maximum(hits, SEGMENT_TOKENS).astype(F32)
    factor = adapter_scale / jnp.full((rank, SEGMENT_TOKENS), limit, F32)
    grad_parts = three_parts(low_grad * factor, 0)
    in_parts = three_parts(low_in * factor, 0)
    tbuf[0, :, :feat] = add_parts(
        jnp.dot(grad_parts, tok_ref[...], preferred_element_type=F32), rank
    )
    tbuf[0, :, feat:] = add_parts(
        jnp.dot(in_parts, grad_ref[...], preferred_element_type=F32), rank
    )
    t_copies = []
    for s in range(1, n):
        cp = pltpu.make_async_remote_copy(
            src_ref=tbuf.at[0],
            dst_ref=tbuf.at[s],
            send_sem=t_send.at[s - 1],
            recv_sem=t_recv.at[s - 1],
            device_id={"dp": lax.rem(z + s, n)},
            device_id_type=MESH,
        )
        cp.start()
        t_copies.append(cp)

    left = three_parts(jnp.transpose(adapter_scale * low_grad), 1)
    for i in range(chunks):
        span = pl.ds(i * chunk, chunk)
        down = abuf[from_owner, :, span]
        acc[i] = product(0, i) + jnp.dot(
            left, jnp.concatenate([down, down, down], axis=0), preferred_element_type=F32
        )
    for i in range(chunks):
        total = acc[i]
        for s in range(1, chips):
            p_copies[s, i].wait_recv()
            total = total + prec[s - 1, i]
        out_ref[:, pl.ds(i * chunk, chunk)] = total.astype(BF16)

    for cp in t_copies:
        cp.wait_recv()
    for k in range(per):
        mine = jnp.where(kept == k, 1.0, 0.0).astype(F32)
        gdown_ref[k] = tbuf[from_user, :, :feat] * mine
        gup_ref[k] = tbuf[from_user, :, feat:] * mine

    g_copy.wait_send()
    for group in (a_copies, l_copies, t_copies, w_copies.values(), p_copies.values()):
        for cp in group:
            cp.wait_send()


def on_device(
    n,
    tn,
    entered_tokens,
    output_grad,
    value_matrix,
    adapter_down,
    adapter_up,
    segment_owner_adapter,
    adapter_storage,
):
    tokens, feat = entered_tokens.shape
    cols = output_grad.shape[1]
    per, rank, _ = adapter_down.shape
    assert tokens == SEGMENT_TOKENS and segment_owner_adapter.shape[0] == n
    chips = tn // CORES
    chunk = min(512, feat)
    chunks = feat // chunk
    vmem = pl.BlockSpec(memory_space=pltpu.VMEM)
    dma = pltpu.SemaphoreType.DMA
    return pl.pallas_call(
        functools.partial(kernel, n, tn, chunk),
        out_shape=(
            jax.ShapeDtypeStruct((tokens, feat), BF16),
            jax.ShapeDtypeStruct((per, rank, feat), F32),
            jax.ShapeDtypeStruct((per, rank, cols), F32),
        ),
        in_specs=[pl.BlockSpec(memory_space=pl.ANY)] * 7,
        out_specs=(vmem, vmem, vmem),
        scratch_shapes=[
            pltpu.SMEM(segment_owner_adapter.shape, jnp.int32),
            pltpu.SMEM(adapter_storage.shape, jnp.int32),
            pltpu.VMEM(entered_tokens.shape, BF16),
            pltpu.VMEM(output_grad.shape, BF16),
            pltpu.VMEM(adapter_down.shape, BF16),
            pltpu.VMEM(adapter_up.shape, BF16),
            dma((6,)),
            pltpu.VMEM((chips, feat, cols), BF16),
            pltpu.VMEM((chips, feat, cols), BF16),
            pltpu.VMEM((tokens, cols), BF16),
            pltpu.VMEM((n, rank, feat + cols), BF16),
            pltpu.VMEM((tn, 2 * rank, tokens), F32),
            pltpu.VMEM((n, rank, feat + cols), F32),
            pltpu.VMEM((chips - 1, chunks, tokens, chunk), F32),
            pltpu.VMEM((chips - 1, chunks, tokens, chunk), F32),
            pltpu.VMEM((chunks, tokens, chunk), F32),
            dma((chips, chunks)),
            dma((chips, chunks)),
            dma((chips, chunks)),
            dma((2,)),
            dma((n - 1,)),
            dma((n - 1,)),
            dma((tn - 1,)),
            dma((tn - 1,)),
            dma((n - 1,)),
            dma((n - 1,)),
            dma((chips - 1, chunks)),
            dma((chips - 1, chunks)),
        ],
        compiler_params=pltpu.CompilerParams(
            collective_id=0, has_side_effects=True, vmem_limit_bytes=VMEM_LIMIT
        ),
        cost_estimate=pl.CostEstimate(
            flops=2 * tokens * feat * cols * tn, bytes_accessed=2 * value_matrix.size, transcendentals=0
        ),
    )(
        segment_owner_adapter,
        adapter_storage,
        entered_tokens,
        output_grad,
        value_matrix,
        adapter_down,
        adapter_up,
    )


def solution(mesh):
    in_specs = (
        P(("groups", "dp"), "tensor"),
        P(("groups", "dp"), "tensor"),
        P(None, "tensor"),
        P(("groups", "dp"), None, "tensor"),
        P(("groups", "dp"), None, "tensor"),
        P("groups"),
        P("groups"),
    )
    out_specs = (
        P(("groups", "dp"), "tensor"),
        P(("groups", "dp"), None, "tensor"),
        P(("groups", "dp"), None, "tensor"),
    )
    body = functools.partial(on_device, mesh.shape["dp"], mesh.shape["tensor"])
    return jax.shard_map(
        body, mesh=mesh, in_specs=in_specs, out_specs=out_specs, check_vma=False
    )
```

```python
import functools

import jax
import jax.numpy as jnp
from jax import lax
from jax.experimental import pallas as pl
from jax.experimental.pallas import tpu as pltpu
from jax.sharding import PartitionSpec as P

SEGMENT_TOKENS = 128
CORES = 2
adapter_scale = 2.0
VMEM_LIMIT = 60 * 1024 * 1024
EARLY = 2
LATE = 2
MESH = pl.DeviceIdType.MESH
F32 = jnp.float32
BF16 = jnp.bfloat16


def dot_last(a, b):
    return lax.dot_general(a, b, (((1,), (1,)), ((), ())), preferred_element_type=F32)


def three_parts(x, axis):
    high = x.astype(BF16)
    rest = x - high.astype(F32)
    mid = rest.astype(BF16)
    low = (rest - mid.astype(F32)).astype(BF16)
    return jnp.concatenate([high, mid, low], axis=axis)


def add_parts(x, rows):
    return x[:rows] + x[rows : 2 * rows] + x[2 * rows :]


def kernel(
    n,
    tn,
    chunk,
    seg_hbm,
    store_hbm,
    tok_hbm,
    grad_hbm,
    w_ref,
    down_hbm,
    up_hbm,
    out_ref,
    gdown_ref,
    gup_ref,
    seg_ref,
    store_ref,
    tok_ref,
    grad_ref,
    down_ref,
    up_ref,
    in_sem,
    w_mine,
    w_sib,
    g_sib,
    dbuf,
    ubuf,
    lbuf,
    dterm,
    uterm,
    psend,
    prec,
    acc,
    w_sem,
    ws_send,
    ws_recv,
    g_sem,
    a_send,
    a_recv,
    l_send,
    l_recv,
    t_send,
    t_recv,
    p_send,
    p_recv,
):
    per, rank, feat = down_ref.shape
    cols = up_ref.shape[2]
    chips = tn // CORES
    chunks = feat // chunk
    z = lax.axis_index("dp")
    j = lax.axis_index("tensor")
    x = j // CORES
    c = lax.rem(j, CORES)
    sib = x * CORES + (1 - c)

    def w_rows(chip, core, i):
        start = (chip * CORES + core) * feat + i * chunk
        return w_ref.at[pl.ds(pl.multiple_of(start, chunk), chunk)]

    loads = [
        pltpu.make_async_copy(src, dst, in_sem.at[k])
        for k, (src, dst) in enumerate(
            (
                (seg_hbm, seg_ref),
                (store_hbm, store_ref),
                (down_hbm, down_ref),
                (up_hbm, up_ref),
                (grad_hbm, grad_ref),
                (tok_hbm, tok_ref),
            )
        )
    ]
    for cp in loads:
        cp.start()

    steps = [(s, i) for s in list(range(1, chips)) + [0] for i in range(chunks)]

    w_local = {}
    for s, i in steps:
        chip = lax.rem(x + s, chips)
        w_local[s, i] = pltpu.make_async_copy(
            w_rows(chip, c, i), w_mine.at[s, pl.ds(i * chunk, chunk)], w_sem.at[s, i]
        )
        w_local[s, i].start()

    barrier = pltpu.get_barrier_semaphore()
    for s in range(1, tn):
        pl.semaphore_signal(
            barrier, inc=1, device_id={"tensor": lax.rem(j + s, tn)}, device_id_type=MESH
        )
    for s in range(1, n):
        pl.semaphore_signal(
            barrier, inc=1, device_id={"dp": lax.rem(z + s, n)}, device_id_type=MESH
        )

    for cp in loads[:4]:
        cp.wait()
    my_slot = store_ref[seg_ref[z]]
    my_owner = my_slot // per
    kept = jnp.int32(0)
    user = jnp.int32(0)
    hits = jnp.int32(0)
    for s in range(n):
        slot = store_ref[seg_ref[s]]
        here = slot // per == z
        kept = jnp.where(here, lax.rem(slot, per), kept)
        user = jnp.where(here, s, user)
        hits = hits + jnp.where(seg_ref[s] == seg_ref[z], SEGMENT_TOKENS, 0)
    from_owner = lax.rem(z - my_owner + n, n)
    from_user = lax.rem(z - user + n, n)

    ubuf[0] = up_ref[kept]
    dbuf[0] = down_ref[kept]

    pl.semaphore_wait(barrier, (tn - 1) + (n - 1))

    def to_all(axis, count, buf, send_sem, recv_sem):
        me = lax.axis_index(axis)
        copies = []
        for s in range(1, count):
            cp = pltpu.make_async_remote_copy(
                src_ref=buf.at[0],
                dst_ref=buf.at[s],
                send_sem=send_sem.at[s - 1],
                recv_sem=recv_sem.at[s - 1],
                device_id={axis: lax.rem(me + s, count)},
                device_id_type=MESH,
            )
            cp.start()
            copies.append(cp)
        return copies

    def arrive(copies):
        for cp in copies:
            cp.wait_recv()

    def total_of(buf, count):
        total = buf[0]
        for s in range(1, count):
            total = total + buf[s]
        return total

    up_copies = to_all("dp", n, ubuf, a_send.at[0], a_recv.at[0])
    loads[4].wait()
    g_copy = pltpu.make_async_remote_copy(
        src_ref=grad_ref,
        dst_ref=g_sib,
        send_sem=g_sem.at[0],
        recv_sem=g_sem.at[1],
        device_id={"tensor": sib},
        device_id_type=MESH,
    )
    g_copy.start()
    w_copies = {}
    for s, i in steps:
        chip = lax.rem(x + s, chips)
        cp = pltpu.make_async_remote_copy(
            src_ref=w_rows(chip, 1 - c, i),
            dst_ref=w_sib.at[s, pl.ds(i * chunk, chunk)],
            send_sem=ws_send.at[s, i],
            recv_sem=ws_recv.at[s, i],
            device_id={"tensor": sib},
            device_id_type=MESH,
        )
        cp.start()
        w_copies[s, i] = cp
    down_copies = to_all("dp", n, dbuf, a_send.at[1], a_recv.at[1])

    def product(s, i):
        w_local[s, i].wait()
        w_copies[s, i].wait_recv()
        rows = pl.ds(i * chunk, chunk)
        return dot_last(grad_ref[...], w_mine[s, rows]) + dot_last(g_sib[...], w_sib[s, rows])

    p_copies = {}

    def send_partial(s, i):
        psend[s - 1, i] = product(s, i)
        cp = pltpu.make_async_remote_copy(
            src_ref=psend.at[s - 1, i],
            dst_ref=prec.at[s - 1, i],
            send_sem=p_send.at[s - 1, i],
            recv_sem=p_recv.at[s - 1, i],
            device_id={"tensor": lax.rem(x + s, chips) * CORES + c},
            device_id_type=MESH,
        )
        cp.start()
        p_copies[s, i] = cp

    partials = [(s, i) for s, i in steps if s > 0]
    limit = jnp.maximum(hits, SEGMENT_TOKENS).astype(F32)
    factor = adapter_scale / jnp.full((rank, SEGMENT_TOKENS), limit, F32)

    arrive(up_copies)
    lbuf[0, 0] = dot_last(ubuf[from_owner], grad_ref[...])
    lg_copies = to_all("tensor", tn, lbuf.at[0], l_send.at[0], l_recv.at[0])
    g_copy.wait_recv()
    for s, i in partials[:EARLY]:
        send_partial(s, i)
    loads[5].wait()
    arrive(lg_copies)
    low_grad = total_of(lbuf.at[0], tn)
    dterm[0] = add_parts(
        jnp.dot(three_parts(low_grad * factor, 0), tok_ref[...], preferred_element_type=F32), rank
    )
    dt_copies = to_all("dp", n, dterm, t_send.at[0], t_recv.at[0])
    for s, i in partials[EARLY:LATE]:
        send_partial(s, i)

    arrive(down_copies)
    lbuf[1, 0] = dot_last(dbuf[from_owner], tok_ref[...])
    li_copies = to_all("tensor", tn, lbuf.at[1], l_send.at[1], l_recv.at[1])
    for s, i in partials[LATE:]:
        send_partial(s, i)
    arrive(li_copies)
    uterm[0] = add_parts(
        jnp.dot(
            three_parts(total_of(lbuf.at[1], tn) * factor, 0),
            grad_ref[...],
            preferred_element_type=F32,
        ),
        rank,
    )
    ut_copies = to_all("dp", n, uterm, t_send.at[1], t_recv.at[1])

    left = three_parts(jnp.transpose(adapter_scale * low_grad), 1)
    for i in range(chunks):
        span = pl.ds(i * chunk, chunk)
        down = dbuf[from_owner, :, span]
        acc[i] = product(0, i) + jnp.dot(
            left, jnp.concatenate([down, down, down], axis=0), preferred_element_type=F32
        )
    for i in range(chunks):
        total = acc[i]
        for s in range(1, chips):
            p_copies[s, i].wait_recv()
            total = total + prec[s - 1, i]
        out_ref[:, pl.ds(i * chunk, chunk)] = total.astype(BF16)

    arrive(dt_copies)
    arrive(ut_copies)
    for k in range(per):
        mine = jnp.where(kept == k, 1.0, 0.0).astype(F32)
        gdown_ref[k] = dterm[from_user] * mine
        gup_ref[k] = uterm[from_user] * mine

    g_copy.wait_send()
    for group in (
        up_copies,
        down_copies,
        lg_copies,
        li_copies,
        dt_copies,
        ut_copies,
        w_copies.values(),
        p_copies.values(),
    ):
        for cp in group:
            cp.wait_send()


def write_out(a, b, c, a_out, b_out, c_out, a_held, b_held, c_held, sem):
    rows = ((a, a_held, a_out), (b, b_held, b_out), (c, c_held, c_out))
    loads = [pltpu.make_async_copy(r[0], r[1], sem.at[0, k]) for k, r in enumerate(rows)]
    stores = [pltpu.make_async_copy(r[1], r[2], sem.at[1, k]) for k, r in enumerate(rows)]
    for cp in loads:
        cp.start()
    for load, store in zip(loads, stores):
        load.wait()
        store.start()
    for cp in stores:
        cp.wait()


def on_device(
    n,
    tn,
    entered_tokens,
    output_grad,
    value_matrix,
    adapter_down,
    adapter_up,
    segment_owner_adapter,
    adapter_storage,
):
    tokens, feat = entered_tokens.shape
    cols = output_grad.shape[1]
    per, rank, _ = adapter_down.shape
    assert tokens == SEGMENT_TOKENS and segment_owner_adapter.shape[0] == n
    chips = tn // CORES
    chunk = min(512, feat)
    chunks = feat // chunk
    vmem = pl.BlockSpec(memory_space=pltpu.VMEM)
    dma = pltpu.SemaphoreType.DMA
    results = pl.pallas_call(
        functools.partial(kernel, n, tn, chunk),
        out_shape=(
            jax.ShapeDtypeStruct((tokens, feat), BF16),
            jax.ShapeDtypeStruct((per, rank, feat), F32),
            jax.ShapeDtypeStruct((per, rank, cols), F32),
        ),
        in_specs=[pl.BlockSpec(memory_space=pltpu.HBM)] * 7,
        out_specs=(vmem, vmem, vmem),
        scratch_shapes=[
            pltpu.SMEM(segment_owner_adapter.shape, jnp.int32),
            pltpu.SMEM(adapter_storage.shape, jnp.int32),
            pltpu.VMEM(entered_tokens.shape, BF16),
            pltpu.VMEM(output_grad.shape, BF16),
            pltpu.VMEM(adapter_down.shape, BF16),
            pltpu.VMEM(adapter_up.shape, BF16),
            dma((6,)),
            pltpu.VMEM((chips, feat, cols), BF16),
            pltpu.VMEM((chips, feat, cols), BF16),
            pltpu.VMEM((tokens, cols), BF16),
            pltpu.VMEM((n, rank, feat), BF16),
            pltpu.VMEM((n, rank, cols), BF16),
            pltpu.VMEM((2, tn, rank, tokens), F32),
            pltpu.VMEM((n, rank, feat), F32),
            pltpu.VMEM((n, rank, cols), F32),
            pltpu.VMEM((chips - 1, chunks, tokens, chunk), F32),
            pltpu.VMEM((chips - 1, chunks, tokens, chunk), F32),
            pltpu.VMEM((chunks, tokens, chunk), F32),
            dma((chips, chunks)),
            dma((chips, chunks)),
            dma((chips, chunks)),
            dma((2,)),
            dma((2, n - 1)),
            dma((2, n - 1)),
            dma((2, tn - 1)),
            dma((2, tn - 1)),
            dma((2, n - 1)),
            dma((2, n - 1)),
            dma((chips - 1, chunks)),
            dma((chips - 1, chunks)),
        ],
        compiler_params=pltpu.CompilerParams(
            collective_id=0, has_side_effects=True, vmem_limit_bytes=VMEM_LIMIT
        ),
        cost_estimate=pl.CostEstimate(
            flops=2 * tokens * feat * cols * tn, bytes_accessed=2 * value_matrix.size, transcendentals=0
        ),
    )(
        segment_owner_adapter,
        adapter_storage,
        entered_tokens,
        output_grad,
        value_matrix,
        adapter_down,
        adapter_up,
    )
    return pl.pallas_call(
        write_out,
        out_shape=tuple(jax.ShapeDtypeStruct(r.shape, r.dtype) for r in results),
        in_specs=[pl.BlockSpec(memory_space=pl.ANY)] * 3,
        out_specs=(pl.BlockSpec(memory_space=pl.ANY),) * 3,
        scratch_shapes=[pltpu.VMEM(r.shape, r.dtype) for r in results] + [dma((2, 3))],
        compiler_params=pltpu.CompilerParams(vmem_limit_bytes=VMEM_LIMIT),
    )(*results)


def solution(mesh):
    in_specs = (
        P(("groups", "dp"), "tensor"),
        P(("groups", "dp"), "tensor"),
        P(None, "tensor"),
        P(("groups", "dp"), None, "tensor"),
        P(("groups", "dp"), None, "tensor"),
        P("groups"),
        P("groups"),
    )
    out_specs = (
        P(("groups", "dp"), "tensor"),
        P(("groups", "dp"), None, "tensor"),
        P(("groups", "dp"), None, "tensor"),
    )
    body = functools.partial(on_device, mesh.shape["dp"], mesh.shape["tensor"])
    return jax.shard_map(
        body, mesh=mesh, in_specs=in_specs, out_specs=out_specs, check_vma=False
    )
```

```python
import functools

import jax
import jax.numpy as jnp
from jax import lax
from jax.experimental import pallas as pl
from jax.experimental.pallas import tpu as pltpu
from jax.sharding import PartitionSpec as P

SEGMENT_TOKENS = 128
CORES = 2
adapter_scale = 2.0
VMEM_LIMIT = 60 * 1024 * 1024
HALVES = 2
SHARED = 2
EARLY = 0
LATE = 1
MESH = pl.DeviceIdType.MESH
F32 = jnp.float32
BF16 = jnp.bfloat16


def dot_last(a, b):
    return lax.dot_general(a, b, (((1,), (1,)), ((), ())), preferred_element_type=F32)


def three_parts(x, axis):
    high = x.astype(BF16)
    rest = x - high.astype(F32)
    mid = rest.astype(BF16)
    low = (rest - mid.astype(F32)).astype(BF16)
    return jnp.concatenate([high, mid, low], axis=axis)


def add_parts(x, rows):
    return x[:rows] + x[rows : 2 * rows] + x[2 * rows :]


def kernel(
    n,
    tn,
    chunk,
    shared,
    seg_hbm,
    store_hbm,
    tok_hbm,
    grad_hbm,
    w_ref,
    down_hbm,
    up_hbm,
    out_ref,
    gdown_ref,
    gup_ref,
    seg_ref,
    store_ref,
    tok_ref,
    grad_ref,
    down_ref,
    up_ref,
    in_sem,
    w_mine,
    w_sib,
    g_sib,
    dbuf,
    dstage,
    ubuf,
    lbuf,
    dterm,
    tstage,
    uterm,
    wx,
    gx,
    psend,
    prec,
    acc,
    w_sem,
    ws_send,
    ws_recv,
    g_sem,
    a_send,
    a_recv,
    l_send,
    l_recv,
    t_send,
    t_recv,
    p_send,
    p_recv,
    d_sem,
    dt_sem,
    x_sem,
    hop_sem,
    gx_sem,
):
    per, rank, feat = down_ref.shape
    cols = up_ref.shape[2]
    chips = tn // CORES
    chunks = feat // chunk
    z = lax.axis_index("dp")
    j = lax.axis_index("tensor")
    x = j // CORES
    c = lax.rem(j, CORES)
    sib = x * CORES + (1 - c)
    y = lax.axis_index("groups")
    z_near = z + 1 - 2 * lax.rem(z, 2)
    z_far = lax.rem(z + 2, n)
    half = feat // HALVES

    def w_rows(chip, core, i):
        start = (chip * CORES + core) * feat + i * chunk
        return w_ref.at[pl.ds(pl.multiple_of(start, chunk), chunk)]

    loads = [
        pltpu.make_async_copy(src, dst, in_sem.at[k])
        for k, (src, dst) in enumerate(
            (
                (seg_hbm, seg_ref),
                (store_hbm, store_ref),
                (down_hbm, down_ref),
                (up_hbm, up_ref),
                (grad_hbm, grad_ref),
                (tok_hbm, tok_ref),
            )
        )
    ]
    for cp in loads:
        cp.start()

    steps = [(s, i) for s in range(1, chips) for i in range(shared, chunks)]
    steps += [(0, i) for i in range(chunks)]

    w_local = {}
    for s, i in steps:
        chip = lax.rem(x + s, chips)
        w_local[s, i] = pltpu.make_async_copy(
            w_rows(chip, c, i), w_mine.at[s, pl.ds(i * chunk, chunk)], w_sem.at[s, i]
        )
        w_local[s, i].start()

    barrier = pltpu.get_barrier_semaphore()
    for s in range(1, tn):
        pl.semaphore_signal(
            barrier, inc=1, device_id={"tensor": lax.rem(j + s, tn)}, device_id_type=MESH
        )
    for s in range(1, n):
        pl.semaphore_signal(
            barrier, inc=1, device_id={"dp": lax.rem(z + s, n)}, device_id_type=MESH
        )

    if shared:
        pl.semaphore_signal(barrier, inc=1, device_id={"groups": 1 - y}, device_id_type=MESH)

    for cp in loads[:4]:
        cp.wait()
    my_slot = store_ref[seg_ref[z]]
    my_owner = my_slot // per
    kept = jnp.int32(0)
    user = jnp.int32(0)
    hits = jnp.int32(0)
    near_user = jnp.int32(0)
    near_owner = store_ref[seg_ref[z_near]] // per
    for s in range(n):
        slot = store_ref[seg_ref[s]]
        here = slot // per == z
        kept = jnp.where(here, lax.rem(slot, per), kept)
        user = jnp.where(here, s, user)
        near_user = jnp.where(slot // per == z_near, s, near_user)
        hits = hits + jnp.where(seg_ref[s] == seg_ref[z], SEGMENT_TOKENS, 0)
    from_owner = lax.rem(z - my_owner + n, n)
    from_user = lax.rem(z - user + n, n)

    ubuf[0] = up_ref[kept]
    own_down = down_ref[kept]
    for h in range(HALVES):
        dbuf[h, 0] = own_down[:, h * half : (h + 1) * half]

    pl.semaphore_wait(barrier, (tn - 1) + (n - 1) + (1 if shared else 0))

    def remote(src, dst, send_sem, recv_sem, device_id):
        cp = pltpu.make_async_remote_copy(
            src_ref=src,
            dst_ref=dst,
            send_sem=send_sem,
            recv_sem=recv_sem,
            device_id=device_id,
            device_id_type=MESH,
        )
        cp.start()
        return cp

    routed = []

    def route_first(buf, sem, h):
        if n == 4:
            out = [remote(buf.at[h, 0], buf.at[h, 1], sem.at[0, h, 0], sem.at[1, h, 0], {"dp": z_far})]
        else:
            out = [
                remote(
                    buf.at[h, 0],
                    buf.at[h, s],
                    sem.at[0, h, s - 1],
                    sem.at[1, h, s - 1],
                    {"dp": lax.rem(z + s, n)},
                )
                for s in range(1, n)
            ]
        routed.extend(out)
        return out

    def route_second(buf, stage, sem, h, first, near_wants):
        if n != 4:
            return first
        arrive(first)
        stage[h] = jnp.where(near_wants == z_far, buf[h, 1], buf[h, 0])
        cp = remote(stage.at[h], buf.at[h, 2], sem.at[0, h, 1], sem.at[1, h, 1], {"dp": z_near})
        routed.append(cp)
        return [cp]

    def route_pick(buf, h, source):
        if n == 4:
            other = jnp.where(source == z_far, buf[h, 1], buf[h, 2])
            return jnp.where(source == z, buf[h, 0], other)
        return buf[h, lax.rem(z - source + n, n)]

    def to_all(axis, count, buf, send_sem, recv_sem):
        me = lax.axis_index(axis)
        copies = []
        for s in range(1, count):
            cp = pltpu.make_async_remote_copy(
                src_ref=buf.at[0],
                dst_ref=buf.at[s],
                send_sem=send_sem.at[s - 1],
                recv_sem=recv_sem.at[s - 1],
                device_id={axis: lax.rem(me + s, count)},
                device_id_type=MESH,
            )
            cp.start()
            copies.append(cp)
        return copies

    def arrive(copies):
        for cp in copies:
            cp.wait_recv()

    def total_of(buf, count):
        total = buf[0]
        for s in range(1, count):
            total = total + buf[s]
        return total

    up_copies = to_all("dp", n, ubuf, a_send.at[0], a_recv.at[0])
    loads[4].wait()

    share_copies = []
    if shared:
        quarter = shared * chunk // 4
        mine = y * 2 + lax.rem(z, 2)
        across = (1 - y) * 2 + lax.rem(z, 2)
        beside = y * 2 + 1 - lax.rem(z, 2)
        x_copies = []
        for r in range(CORES):
            core = c if r == 0 else 1 - c
            start = ((1 - x) * CORES + core) * feat + mine * quarter
            x_copies.append(
                remote(
                    w_ref.at[pl.ds(pl.multiple_of(start, quarter), quarter)],
                    wx.at[r, mine],
                    x_sem.at[0, r],
                    x_sem.at[1, r],
                    {"tensor": (1 - x) * CORES + core},
                )
            )
        gx_copy = remote(
            grad_ref, gx.at[0], gx_sem.at[0, 0], gx_sem.at[1, 0], {"tensor": (1 - x) * CORES + c}
        )
        share_copies += x_copies + [gx_copy]
    g_copy = pltpu.make_async_remote_copy(
        src_ref=grad_ref,
        dst_ref=g_sib,
        send_sem=g_sem.at[0],
        recv_sem=g_sem.at[1],
        device_id={"tensor": sib},
        device_id_type=MESH,
    )
    g_copy.start()
    down_first = [route_first(dbuf, d_sem, h) for h in range(HALVES)]
    w_copies = {}
    for s, i in steps:
        chip = lax.rem(x + s, chips)
        cp = pltpu.make_async_remote_copy(
            src_ref=w_rows(chip, 1 - c, i),
            dst_ref=w_sib.at[s, pl.ds(i * chunk, chunk)],
            send_sem=ws_send.at[s, i],
            recv_sem=ws_recv.at[s, i],
            device_id={"tensor": sib},
            device_id_type=MESH,
        )
        cp.start()
        w_copies[s, i] = cp
    def product(s, i):
        w_local[s, i].wait()
        w_copies[s, i].wait_recv()
        rows = pl.ds(i * chunk, chunk)
        return dot_last(grad_ref[...], w_mine[s, rows]) + dot_last(g_sib[...], w_sib[s, rows])

    p_copies = {}

    def send_partial(s, i):
        psend[s - 1, i] = product(s, i)
        cp = pltpu.make_async_remote_copy(
            src_ref=psend.at[s - 1, i],
            dst_ref=prec.at[s - 1, i],
            send_sem=p_send.at[s - 1, i],
            recv_sem=p_recv.at[s - 1, i],
            device_id={"tensor": lax.rem(x + s, chips) * CORES + c},
            device_id_type=MESH,
        )
        cp.start()
        p_copies[s, i] = cp

    partials = [(s, i) for s, i in steps if s > 0]
    limit = jnp.maximum(hits, SEGMENT_TOKENS).astype(F32)
    factor = adapter_scale / jnp.full((rank, SEGMENT_TOKENS), limit, F32)

    arrive(up_copies)
    lbuf[0, 0] = dot_last(ubuf[from_owner], grad_ref[...])
    lg_copies = to_all("tensor", tn, lbuf.at[0], l_send.at[0], l_recv.at[0])
    g_copy.wait_recv()
    for s, i in partials[:EARLY]:
        send_partial(s, i)
    down_second = [
        route_second(dbuf, dstage, d_sem, h, down_first[h], near_owner) for h in range(HALVES)
    ]
    if shared:
        z_copies = []
        y_copies = []
        for r in range(CORES):
            x_copies[r].wait_recv()
            block = wx.at[r, mine]
            z_copies.append(
                remote(block, block, hop_sem.at[0, 0, r], hop_sem.at[1, 0, r], {"dp": z_near})
            )
            y_copies.append(
                remote(block, block, hop_sem.at[0, 1, r], hop_sem.at[1, 1, r], {"groups": 1 - y})
            )
        gx_copy.wait_recv()
        gx_other = remote(
            gx.at[0], gx.at[1], gx_sem.at[0, 1], gx_sem.at[1, 1], {"tensor": sib}
        )
        share_copies += z_copies + y_copies + [gx_other]
    loads[5].wait()
    arrive(lg_copies)
    low_grad = total_of(lbuf.at[0], tn)
    grad_parts = three_parts(low_grad * factor, 0)
    term_first = []
    for h in range(HALVES):
        dterm[h, 0] = add_parts(
            jnp.dot(
                grad_parts, tok_ref[:, pl.ds(h * half, half)], preferred_element_type=F32
            ),
            rank,
        )
        term_first.append(route_first(dterm, dt_sem, h))
    for s, i in partials[EARLY:LATE]:
        send_partial(s, i)
    if shared:
        z_copies[0].wait_recv()
        block = wx.at[0, beside]
        last_y = remote(block, block, hop_sem.at[0, 2, 0], hop_sem.at[1, 2, 0], {"groups": 1 - y})
        y_copies[1].wait_recv()
        block = wx.at[1, across]
        last_z = remote(block, block, hop_sem.at[0, 2, 1], hop_sem.at[1, 2, 1], {"dp": z_near})
        share_copies += [last_y, last_z]

    for copies in down_second:
        arrive(copies)
    down = [route_pick(dbuf, h, my_owner) for h in range(HALVES)]
    lbuf[1, 0] = sum(
        dot_last(down[h], tok_ref[:, pl.ds(h * half, half)]) for h in range(HALVES)
    )
    li_copies = to_all("tensor", tn, lbuf.at[1], l_send.at[1], l_recv.at[1])
    for s, i in partials[LATE:]:
        send_partial(s, i)
    term_second = [
        route_second(dterm, tstage, dt_sem, h, term_first[h], near_user) for h in range(HALVES)
    ]
    arrive(li_copies)
    uterm[0] = add_parts(
        jnp.dot(
            three_parts(total_of(lbuf.at[1], tn) * factor, 0),
            grad_ref[...],
            preferred_element_type=F32,
        ),
        rank,
    )
    ut_copies = to_all("dp", n, uterm, t_send.at[1], t_recv.at[1])

    left = three_parts(jnp.transpose(adapter_scale * low_grad), 1)
    whole_down = jnp.concatenate(down, axis=1)
    for i in range(chunks):
        part = whole_down[:, i * chunk : (i + 1) * chunk]
        acc[i] = product(0, i) + jnp.dot(
            left, jnp.concatenate([part, part, part], axis=0), preferred_element_type=F32
        )
    for copies in term_second:
        arrive(copies)
    arrive(ut_copies)
    for k in range(per):
        here = jnp.where(kept == k, 1.0, 0.0).astype(F32)
        for h in range(HALVES):
            gdown_ref[k, :, pl.ds(h * half, half)] = route_pick(dterm, h, user) * here
        gup_ref[k] = uterm[from_user] * here
    if shared:
        gx_other.wait_recv()
        arrive([y_copies[0], z_copies[1], last_y, last_z])
        per_chunk = 4 // shared
        for i in range(shared):
            total = acc[i]
            for r in range(CORES):
                rows = jnp.concatenate(
                    [wx[r, q] for q in range(i * per_chunk, (i + 1) * per_chunk)], axis=0
                )
                total = total + dot_last(gx[r], rows)
            out_ref[:, pl.ds(i * chunk, chunk)] = total.astype(BF16)
    for i in range(shared, chunks):
        total = acc[i]
        for s in range(1, chips):
            p_copies[s, i].wait_recv()
            total = total + prec[s - 1, i]
        out_ref[:, pl.ds(i * chunk, chunk)] = total.astype(BF16)

    g_copy.wait_send()
    for group in (
        up_copies,
        routed,
        share_copies,
        lg_copies,
        li_copies,
        ut_copies,
        w_copies.values(),
        p_copies.values(),
    ):
        for cp in group:
            cp.wait_send()


def write_out(a, b, c, a_out, b_out, c_out, a_held, b_held, c_held, sem):
    rows = ((a, a_held, a_out), (b, b_held, b_out), (c, c_held, c_out))
    loads = [pltpu.make_async_copy(r[0], r[1], sem.at[0, k]) for k, r in enumerate(rows)]
    stores = [pltpu.make_async_copy(r[1], r[2], sem.at[1, k]) for k, r in enumerate(rows)]
    for cp in loads:
        cp.start()
    for load, store in zip(loads, stores):
        load.wait()
        store.start()
    for cp in stores:
        cp.wait()


def on_device(
    groups,
    n,
    tn,
    entered_tokens,
    output_grad,
    value_matrix,
    adapter_down,
    adapter_up,
    segment_owner_adapter,
    adapter_storage,
):
    tokens, feat = entered_tokens.shape
    cols = output_grad.shape[1]
    per, rank, _ = adapter_down.shape
    assert tokens == SEGMENT_TOKENS and segment_owner_adapter.shape[0] == n
    chips = tn // CORES
    chunk = min(512, feat)
    chunks = feat // chunk
    shared = SHARED if chips == 2 and groups == 2 and n % 2 == 0 and chunks > SHARED else 0
    quarter = max(shared * chunk // 4, 16)
    vmem = pl.BlockSpec(memory_space=pltpu.VMEM)
    dma = pltpu.SemaphoreType.DMA
    results = pl.pallas_call(
        functools.partial(kernel, n, tn, chunk, shared),
        out_shape=(
            jax.ShapeDtypeStruct((tokens, feat), BF16),
            jax.ShapeDtypeStruct((per, rank, feat), F32),
            jax.ShapeDtypeStruct((per, rank, cols), F32),
        ),
        in_specs=[pl.BlockSpec(memory_space=pltpu.HBM)] * 7,
        out_specs=(vmem, vmem, vmem),
        scratch_shapes=[
            pltpu.SMEM(segment_owner_adapter.shape, jnp.int32),
            pltpu.SMEM(adapter_storage.shape, jnp.int32),
            pltpu.VMEM(entered_tokens.shape, BF16),
            pltpu.VMEM(output_grad.shape, BF16),
            pltpu.VMEM(adapter_down.shape, BF16),
            pltpu.VMEM(adapter_up.shape, BF16),
            dma((6,)),
            pltpu.VMEM((chips, feat, cols), BF16),
            pltpu.VMEM((chips, feat, cols), BF16),
            pltpu.VMEM((tokens, cols), BF16),
            pltpu.VMEM((HALVES, n, rank, feat // HALVES), BF16),
            pltpu.VMEM((HALVES, rank, feat // HALVES), BF16),
            pltpu.VMEM((n, rank, cols), BF16),
            pltpu.VMEM((2, tn, rank, tokens), F32),
            pltpu.VMEM((HALVES, n, rank, feat // HALVES), F32),
            pltpu.VMEM((HALVES, rank, feat // HALVES), F32),
            pltpu.VMEM((n, rank, cols), F32),
            pltpu.VMEM((CORES, 4, quarter, cols), BF16),
            pltpu.VMEM((CORES, tokens, cols), BF16),
            pltpu.VMEM((chips - 1, chunks, tokens, chunk), F32),
            pltpu.VMEM((chips - 1, chunks, tokens, chunk), F32),
            pltpu.VMEM((chunks, tokens, chunk), F32),
            dma((chips, chunks)),
            dma((chips, chunks)),
            dma((chips, chunks)),
            dma((2,)),
            dma((2, n - 1)),
            dma((2, n - 1)),
            dma((2, tn - 1)),
            dma((2, tn - 1)),
            dma((2, n - 1)),
            dma((2, n - 1)),
            dma((chips - 1, chunks)),
            dma((chips - 1, chunks)),
            dma((2, HALVES, n)),
            dma((2, HALVES, n)),
            dma((2, CORES)),
            dma((2, 3, CORES)),
            dma((2, 2)),
        ],
        compiler_params=pltpu.CompilerParams(
            collective_id=0, has_side_effects=True, vmem_limit_bytes=VMEM_LIMIT
        ),
        cost_estimate=pl.CostEstimate(
            flops=2 * tokens * feat * cols * tn, bytes_accessed=2 * value_matrix.size, transcendentals=0
        ),
    )(
        segment_owner_adapter,
        adapter_storage,
        entered_tokens,
        output_grad,
        value_matrix,
        adapter_down,
        adapter_up,
    )
    return pl.pallas_call(
        write_out,
        out_shape=tuple(jax.ShapeDtypeStruct(r.shape, r.dtype) for r in results),
        in_specs=[pl.BlockSpec(memory_space=pl.ANY)] * 3,
        out_specs=(pl.BlockSpec(memory_space=pl.ANY),) * 3,
        scratch_shapes=[pltpu.VMEM(r.shape, r.dtype) for r in results] + [dma((2, 3))],
        compiler_params=pltpu.CompilerParams(vmem_limit_bytes=VMEM_LIMIT),
    )(*results)


def solution(mesh):
    in_specs = (
        P(("groups", "dp"), "tensor"),
        P(("groups", "dp"), "tensor"),
        P(None, "tensor"),
        P(("groups", "dp"), None, "tensor"),
        P(("groups", "dp"), None, "tensor"),
        P("groups"),
        P("groups"),
    )
    out_specs = (
        P(("groups", "dp"), "tensor"),
        P(("groups", "dp"), None, "tensor"),
        P(("groups", "dp"), None, "tensor"),
    )
    body = functools.partial(on_device, mesh.shape["groups"], mesh.shape["dp"], mesh.shape["tensor"])
    return jax.shard_map(
        body, mesh=mesh, in_specs=in_specs, out_specs=out_specs, check_vma=False
    )
```

```python
import functools

import jax
import jax.numpy as jnp
from jax import lax
from jax.experimental import pallas as pl
from jax.experimental.pallas import tpu as pltpu
from jax.sharding import PartitionSpec as P

SEGMENT_TOKENS = 128
CORES = 2
adapter_scale = 2.0
VMEM_LIMIT = 60 * 1024 * 1024
HALVES = 2
SHARED = 2
EARLY = 0
LATE = 1
MESH = pl.DeviceIdType.MESH
F32 = jnp.float32
BF16 = jnp.bfloat16


def dot_last(a, b):
    return lax.dot_general(a, b, (((1,), (1,)), ((), ())), preferred_element_type=F32)


def three_parts(x, axis):
    high = x.astype(BF16)
    rest = x - high.astype(F32)
    mid = rest.astype(BF16)
    low = (rest - mid.astype(F32)).astype(BF16)
    return jnp.concatenate([high, mid, low], axis=axis)


def add_parts(x, rows):
    return x[:rows] + x[rows : 2 * rows] + x[2 * rows :]


def kernel(
    n,
    tn,
    chunk,
    shared,
    seg_hbm,
    store_hbm,
    tok_hbm,
    grad_hbm,
    w_ref,
    down_hbm,
    up_hbm,
    out_ref,
    gdown_ref,
    gup_ref,
    seg_ref,
    store_ref,
    tok_ref,
    grad_ref,
    down_ref,
    up_ref,
    in_sem,
    w_mine,
    w_sib,
    g_sib,
    dbuf,
    dstage,
    ubuf,
    lbuf,
    dterm,
    tstage,
    uterm,
    wx,
    gx,
    psend,
    prec,
    acc,
    w_sem,
    ws_send,
    ws_recv,
    g_sem,
    a_send,
    a_recv,
    l_send,
    l_recv,
    t_send,
    t_recv,
    p_send,
    p_recv,
    d_sem,
    dt_sem,
    x_sem,
    hop_sem,
    gx_sem,
):
    per, rank, feat = down_ref.shape
    cols = up_ref.shape[2]
    chips = tn // CORES
    chunks = feat // chunk
    z = lax.axis_index("dp")
    j = lax.axis_index("tensor")
    x = j // CORES
    c = lax.rem(j, CORES)
    sib = x * CORES + (1 - c)
    y = lax.axis_index("groups")
    z_near = z + 1 - 2 * lax.rem(z, 2)
    z_far = lax.rem(z + 2, n)
    half = feat // HALVES

    def w_rows(chip, core, i):
        start = (chip * CORES + core) * feat + i * chunk
        return w_ref.at[pl.ds(pl.multiple_of(start, chunk), chunk)]

    loads = [
        pltpu.make_async_copy(src, dst, in_sem.at[k])
        for k, (src, dst) in enumerate(
            (
                (seg_hbm, seg_ref),
                (store_hbm, store_ref),
                (down_hbm, down_ref),
                (up_hbm, up_ref),
                (grad_hbm, grad_ref),
                (tok_hbm, tok_ref),
            )
        )
    ]
    for cp in loads:
        cp.start()

    steps = [(s, i) for s in range(1, chips) for i in range(shared, chunks)]
    steps += [(0, i) for i in range(chunks)]

    w_local = {}
    for s, i in steps:
        chip = lax.rem(x + s, chips)
        w_local[s, i] = pltpu.make_async_copy(
            w_rows(chip, c, i), w_mine.at[s, pl.ds(i * chunk, chunk)], w_sem.at[s, i]
        )
        w_local[s, i].start()

    barrier = pltpu.get_barrier_semaphore()
    for s in range(1, tn):
        pl.semaphore_signal(
            barrier, inc=1, device_id={"tensor": lax.rem(j + s, tn)}, device_id_type=MESH
        )
    for s in range(1, n):
        pl.semaphore_signal(
            barrier, inc=1, device_id={"dp": lax.rem(z + s, n)}, device_id_type=MESH
        )

    if shared:
        pl.semaphore_signal(barrier, inc=1, device_id={"groups": 1 - y}, device_id_type=MESH)

    for cp in loads[:4]:
        cp.wait()
    my_slot = store_ref[seg_ref[z]]
    my_owner = my_slot // per
    kept = jnp.int32(0)
    user = jnp.int32(0)
    hits = jnp.int32(0)
    near_user = jnp.int32(0)
    near_owner = store_ref[seg_ref[z_near]] // per
    for s in range(n):
        slot = store_ref[seg_ref[s]]
        here = slot // per == z
        kept = jnp.where(here, lax.rem(slot, per), kept)
        user = jnp.where(here, s, user)
        near_user = jnp.where(slot // per == z_near, s, near_user)
        hits = hits + jnp.where(seg_ref[s] == seg_ref[z], SEGMENT_TOKENS, 0)
    from_owner = lax.rem(z - my_owner + n, n)
    from_user = lax.rem(z - user + n, n)

    ubuf[0] = up_ref[kept]
    own_down = down_ref[kept]
    for h in range(HALVES):
        dbuf[h, 0] = own_down[:, h * half : (h + 1) * half]

    pl.semaphore_wait(barrier, (tn - 1) + (n - 1) + (1 if shared else 0))

    def remote(src, dst, send_sem, recv_sem, device_id):
        cp = pltpu.make_async_remote_copy(
            src_ref=src,
            dst_ref=dst,
            send_sem=send_sem,
            recv_sem=recv_sem,
            device_id=device_id,
            device_id_type=MESH,
        )
        cp.start()
        return cp

    routed = []

    def route_first(buf, sem, h):
        if n == 4:
            out = [remote(buf.at[h, 0], buf.at[h, 1], sem.at[0, h, 0], sem.at[1, h, 0], {"dp": z_far})]
        else:
            out = [
                remote(
                    buf.at[h, 0],
                    buf.at[h, s],
                    sem.at[0, h, s - 1],
                    sem.at[1, h, s - 1],
                    {"dp": lax.rem(z + s, n)},
                )
                for s in range(1, n)
            ]
        routed.extend(out)
        return out

    def route_second(buf, stage, sem, h, first, near_wants):
        if n != 4:
            return first
        arrive(first)
        stage[h] = jnp.where(near_wants == z_far, buf[h, 1], buf[h, 0])
        cp = remote(stage.at[h], buf.at[h, 2], sem.at[0, h, 1], sem.at[1, h, 1], {"dp": z_near})
        routed.append(cp)
        return [cp]

    def route_pick(buf, h, source):
        if n == 4:
            other = jnp.where(source == z_far, buf[h, 1], buf[h, 2])
            return jnp.where(source == z, buf[h, 0], other)
        return buf[h, lax.rem(z - source + n, n)]

    def to_all(axis, count, buf, send_sem, recv_sem):
        me = lax.axis_index(axis)
        copies = []
        for s in range(1, count):
            cp = pltpu.make_async_remote_copy(
                src_ref=buf.at[0],
                dst_ref=buf.at[s],
                send_sem=send_sem.at[s - 1],
                recv_sem=recv_sem.at[s - 1],
                device_id={axis: lax.rem(me + s, count)},
                device_id_type=MESH,
            )
            cp.start()
            copies.append(cp)
        return copies

    def arrive(copies):
        for cp in copies:
            cp.wait_recv()

    def total_of(buf, count):
        total = buf[0]
        for s in range(1, count):
            total = total + buf[s]
        return total

    up_copies = to_all("dp", n, ubuf, a_send.at[0], a_recv.at[0])
    loads[4].wait()

    share_copies = []
    if shared:
        quarter = shared * chunk // 4
        mine = y * 2 + lax.rem(z, 2)
        across = (1 - y) * 2 + lax.rem(z, 2)
        beside = y * 2 + 1 - lax.rem(z, 2)

        def share_x(r):
            core = c if r == 0 else 1 - c
            start = ((1 - x) * CORES + core) * feat + mine * quarter
            return remote(
                w_ref.at[pl.ds(pl.multiple_of(start, quarter), quarter)],
                wx.at[r, mine],
                x_sem.at[0, r],
                x_sem.at[1, r],
                {"tensor": (1 - x) * CORES + core},
            )

        x_copies = [share_x(0)]
    g_copy = pltpu.make_async_remote_copy(
        src_ref=grad_ref,
        dst_ref=g_sib,
        send_sem=g_sem.at[0],
        recv_sem=g_sem.at[1],
        device_id={"tensor": sib},
        device_id_type=MESH,
    )
    g_copy.start()
    down_first = [route_first(dbuf, d_sem, h) for h in range(HALVES)]
    w_copies = {}
    for s, i in steps:
        chip = lax.rem(x + s, chips)
        cp = pltpu.make_async_remote_copy(
            src_ref=w_rows(chip, 1 - c, i),
            dst_ref=w_sib.at[s, pl.ds(i * chunk, chunk)],
            send_sem=ws_send.at[s, i],
            recv_sem=ws_recv.at[s, i],
            device_id={"tensor": sib},
            device_id_type=MESH,
        )
        cp.start()
        w_copies[s, i] = cp
    def product(s, i):
        w_local[s, i].wait()
        w_copies[s, i].wait_recv()
        rows = pl.ds(i * chunk, chunk)
        return dot_last(grad_ref[...], w_mine[s, rows]) + dot_last(g_sib[...], w_sib[s, rows])

    p_copies = {}

    def send_partial(s, i):
        psend[s - 1, i] = product(s, i)
        cp = pltpu.make_async_remote_copy(
            src_ref=psend.at[s - 1, i],
            dst_ref=prec.at[s - 1, i],
            send_sem=p_send.at[s - 1, i],
            recv_sem=p_recv.at[s - 1, i],
            device_id={"tensor": lax.rem(x + s, chips) * CORES + c},
            device_id_type=MESH,
        )
        cp.start()
        p_copies[s, i] = cp

    partials = [(s, i) for s, i in steps if s > 0]
    limit = jnp.maximum(hits, SEGMENT_TOKENS).astype(F32)
    factor = adapter_scale / jnp.full((rank, SEGMENT_TOKENS), limit, F32)

    arrive(up_copies)
    lbuf[0, 0] = dot_last(ubuf[from_owner], grad_ref[...])
    lg_copies = to_all("tensor", tn, lbuf.at[0], l_send.at[0], l_recv.at[0])
    if shared:
        x_copies.append(share_x(1))
        gx_copy = remote(
            grad_ref, gx.at[0], gx_sem.at[0, 0], gx_sem.at[1, 0], {"tensor": (1 - x) * CORES + c}
        )
        share_copies += x_copies + [gx_copy]
    g_copy.wait_recv()
    for s, i in partials[:EARLY]:
        send_partial(s, i)
    down_second = [
        route_second(dbuf, dstage, d_sem, h, down_first[h], near_owner) for h in range(HALVES)
    ]
    if shared:
        z_copies = []
        y_copies = []
        for r in range(CORES):
            x_copies[r].wait_recv()
            block = wx.at[r, mine]
            z_copies.append(
                remote(block, block, hop_sem.at[0, 0, r], hop_sem.at[1, 0, r], {"dp": z_near})
            )
            y_copies.append(
                remote(block, block, hop_sem.at[0, 1, r], hop_sem.at[1, 1, r], {"groups": 1 - y})
            )
        gx_copy.wait_recv()
        gx_other = remote(
            gx.at[0], gx.at[1], gx_sem.at[0, 1], gx_sem.at[1, 1], {"tensor": sib}
        )
        share_copies += z_copies + y_copies + [gx_other]
    loads[5].wait()
    arrive(lg_copies)
    low_grad = total_of(lbuf.at[0], tn)
    grad_parts = three_parts(low_grad * factor, 0)
    term_first = []
    for h in range(HALVES):
        dterm[h, 0] = add_parts(
            jnp.dot(
                grad_parts, tok_ref[:, pl.ds(h * half, half)], preferred_element_type=F32
            ),
            rank,
        )
        term_first.append(route_first(dterm, dt_sem, h))
    for s, i in partials[EARLY:LATE]:
        send_partial(s, i)
    if shared:
        z_copies[0].wait_recv()
        block = wx.at[0, beside]
        last_y = remote(block, block, hop_sem.at[0, 2, 0], hop_sem.at[1, 2, 0], {"groups": 1 - y})
        y_copies[1].wait_recv()
        block = wx.at[1, across]
        last_z = remote(block, block, hop_sem.at[0, 2, 1], hop_sem.at[1, 2, 1], {"dp": z_near})
        share_copies += [last_y, last_z]

    for copies in down_second:
        arrive(copies)
    down = [route_pick(dbuf, h, my_owner) for h in range(HALVES)]
    lbuf[1, 0] = sum(
        dot_last(down[h], tok_ref[:, pl.ds(h * half, half)]) for h in range(HALVES)
    )
    li_copies = to_all("tensor", tn, lbuf.at[1], l_send.at[1], l_recv.at[1])
    for s, i in partials[LATE:]:
        send_partial(s, i)
    term_second = [
        route_second(dterm, tstage, dt_sem, h, term_first[h], near_user) for h in range(HALVES)
    ]
    arrive(li_copies)
    uterm[0] = add_parts(
        jnp.dot(
            three_parts(total_of(lbuf.at[1], tn) * factor, 0),
            grad_ref[...],
            preferred_element_type=F32,
        ),
        rank,
    )
    ut_copies = to_all("dp", n, uterm, t_send.at[1], t_recv.at[1])

    left = three_parts(jnp.transpose(adapter_scale * low_grad), 1)
    whole_down = jnp.concatenate(down, axis=1)
    for i in range(chunks):
        part = whole_down[:, i * chunk : (i + 1) * chunk]
        acc[i] = product(0, i) + jnp.dot(
            left, jnp.concatenate([part, part, part], axis=0), preferred_element_type=F32
        )
    for copies in term_second:
        arrive(copies)
    arrive(ut_copies)
    for k in range(per):
        here = jnp.where(kept == k, 1.0, 0.0).astype(F32)
        for h in range(HALVES):
            gdown_ref[k, :, pl.ds(h * half, half)] = route_pick(dterm, h, user) * here
        gup_ref[k] = uterm[from_user] * here
    if shared:
        gx_other.wait_recv()
        arrive([y_copies[0], z_copies[1], last_y, last_z])
        per_chunk = 4 // shared
        for i in range(shared):
            total = acc[i]
            for r in range(CORES):
                rows = jnp.concatenate(
                    [wx[r, q] for q in range(i * per_chunk, (i + 1) * per_chunk)], axis=0
                )
                total = total + dot_last(gx[r], rows)
            out_ref[:, pl.ds(i * chunk, chunk)] = total.astype(BF16)
    for i in range(shared, chunks):
        total = acc[i]
        for s in range(1, chips):
            p_copies[s, i].wait_recv()
            total = total + prec[s - 1, i]
        out_ref[:, pl.ds(i * chunk, chunk)] = total.astype(BF16)

    g_copy.wait_send()
    for group in (
        up_copies,
        routed,
        share_copies,
        lg_copies,
        li_copies,
        ut_copies,
        w_copies.values(),
        p_copies.values(),
    ):
        for cp in group:
            cp.wait_send()


def write_out(a, b, c, a_out, b_out, c_out, sem):
    stores = [
        pltpu.make_async_copy(src, dst, sem.at[k])
        for k, (src, dst) in enumerate(((a, a_out), (b, b_out), (c, c_out)))
    ]
    for cp in stores:
        cp.start()
    for cp in stores:
        cp.wait()


def on_device(
    groups,
    n,
    tn,
    entered_tokens,
    output_grad,
    value_matrix,
    adapter_down,
    adapter_up,
    segment_owner_adapter,
    adapter_storage,
):
    tokens, feat = entered_tokens.shape
    cols = output_grad.shape[1]
    per, rank, _ = adapter_down.shape
    assert tokens == SEGMENT_TOKENS and segment_owner_adapter.shape[0] == n
    chips = tn // CORES
    chunk = min(512, feat)
    chunks = feat // chunk
    shared = SHARED if chips == 2 and groups == 2 and n % 2 == 0 and chunks > SHARED else 0
    quarter = max(shared * chunk // 4, 16)
    vmem = pl.BlockSpec(memory_space=pltpu.VMEM)
    dma = pltpu.SemaphoreType.DMA
    results = pl.pallas_call(
        functools.partial(kernel, n, tn, chunk, shared),
        out_shape=(
            pltpu.VMEM((tokens, feat), BF16),
            pltpu.VMEM((per, rank, feat), F32),
            pltpu.VMEM((per, rank, cols), F32),
        ),
        in_specs=[pl.BlockSpec(memory_space=pltpu.HBM)] * 7,
        out_specs=(vmem, vmem, vmem),
        scratch_shapes=[
            pltpu.SMEM(segment_owner_adapter.shape, jnp.int32),
            pltpu.SMEM(adapter_storage.shape, jnp.int32),
            pltpu.VMEM(entered_tokens.shape, BF16),
            pltpu.VMEM(output_grad.shape, BF16),
            pltpu.VMEM(adapter_down.shape, BF16),
            pltpu.VMEM(adapter_up.shape, BF16),
            dma((6,)),
            pltpu.VMEM((chips, feat, cols), BF16),
            pltpu.VMEM((chips, feat, cols), BF16),
            pltpu.VMEM((tokens, cols), BF16),
            pltpu.VMEM((HALVES, n, rank, feat // HALVES), BF16),
            pltpu.VMEM((HALVES, rank, feat // HALVES), BF16),
            pltpu.VMEM((n, rank, cols), BF16),
            pltpu.VMEM((2, tn, rank, tokens), F32),
            pltpu.VMEM((HALVES, n, rank, feat // HALVES), F32),
            pltpu.VMEM((HALVES, rank, feat // HALVES), F32),
            pltpu.VMEM((n, rank, cols), F32),
            pltpu.VMEM((CORES, 4, quarter, cols), BF16),
            pltpu.VMEM((CORES, tokens, cols), BF16),
            pltpu.VMEM((chips - 1, chunks, tokens, chunk), F32),
            pltpu.VMEM((chips - 1, chunks, tokens, chunk), F32),
            pltpu.VMEM((chunks, tokens, chunk), F32),
            dma((chips, chunks)),
            dma((chips, chunks)),
            dma((chips, chunks)),
            dma((2,)),
            dma((2, n - 1)),
            dma((2, n - 1)),
            dma((2, tn - 1)),
            dma((2, tn - 1)),
            dma((2, n - 1)),
            dma((2, n - 1)),
            dma((chips - 1, chunks)),
            dma((chips - 1, chunks)),
            dma((2, HALVES, n)),
            dma((2, HALVES, n)),
            dma((2, CORES)),
            dma((2, 3, CORES)),
            dma((2, 2)),
        ],
        compiler_params=pltpu.CompilerParams(
            collective_id=0, has_side_effects=True, vmem_limit_bytes=VMEM_LIMIT
        ),
        cost_estimate=pl.CostEstimate(
            flops=2 * tokens * feat * cols * tn, bytes_accessed=2 * value_matrix.size, transcendentals=0
        ),
    )(
        segment_owner_adapter,
        adapter_storage,
        entered_tokens,
        output_grad,
        value_matrix,
        adapter_down,
        adapter_up,
    )
    return pl.pallas_call(
        write_out,
        out_shape=tuple(jax.ShapeDtypeStruct(r.shape, r.dtype) for r in results),
        in_specs=[pl.BlockSpec(memory_space=pl.ANY)] * 3,
        out_specs=(pl.BlockSpec(memory_space=pl.ANY),) * 3,
        scratch_shapes=[dma((3,))],
        compiler_params=pltpu.CompilerParams(vmem_limit_bytes=4 * 1024 * 1024),
    )(*results)


def solution(mesh):
    in_specs = (
        P(("groups", "dp"), "tensor"),
        P(("groups", "dp"), "tensor"),
        P(None, "tensor"),
        P(("groups", "dp"), None, "tensor"),
        P(("groups", "dp"), None, "tensor"),
        P("groups"),
        P("groups"),
    )
    out_specs = (
        P(("groups", "dp"), "tensor"),
        P(("groups", "dp"), None, "tensor"),
        P(("groups", "dp"), None, "tensor"),
    )
    body = functools.partial(on_device, mesh.shape["groups"], mesh.shape["dp"], mesh.shape["tensor"])
    return jax.shard_map(
        body, mesh=mesh, in_specs=in_specs, out_specs=out_specs, check_vma=False
    )
```
